32 devices in a mesh: fsdp: 8 (over z, core), seq: 4 (over y, x).
Axes of the slice: x: 2, y: 2, z: 4, core: 2. Of those that a mesh axis runs over, the one named last changes fastest.
Arguments:
- query_proj: bfloat16 [8, 512, 128], P('fsdp', 'seq'), may hold values from -6 to 6
- key_proj: bfloat16 [8, 512, 128], P('fsdp', 'seq'), may hold values from 0 to 5
- value_proj: bfloat16 [8, 512, 128], P('fsdp', 'seq'), may hold values from 0 to 5
- filters: float32 [128, 128], P('fsdp'), may hold values from -8 to 8
Outputs:
- response: bfloat16 [8, 512, 128], P('fsdp', 'seq')
The draws below stay inside these ranges and needn't reach their ends.
All inputs are finite; a program needn't handle non-finite values.
Results may differ from the reference program's by a relative error of at most 0.012.
Values may be sent and summed in bfloat16 or wider, within the bound.
A program may use at most 64 MiB of HBM per device.

```python
import jax
import jax.numpy as jnp
from jax import lax

CH = 128
TAPS = 128
L = 512
GENOMES = 8


def draw_filters(key, part):
    first, second, third = jax.random.split(jax.random.fold_in(key, 11), 3)
    spans = jnp.exp(jax.random.uniform(first, (CH, 1), minval=jnp.log(0.5 * TAPS), maxval=jnp.log(4.0 * TAPS)))
    steps = jnp.arange(TAPS, dtype=jnp.float32)[None, :]
    signs = 1.0 - 2.0 * (jnp.arange(TAPS) % 2).astype(jnp.float32)[None, :]
    magnitude = 1.0 + 0.5 * jnp.tanh(jax.random.normal(second, (CH, TAPS)))
    scale = jnp.exp(jax.random.uniform(third, (CH, 1), minval=jnp.log(0.5), maxval=jnp.log(2.0)))
    energy = (1.0 - jnp.exp(-2.0 * TAPS / spans)) / (1.0 - jnp.exp(-2.0 / spans))
    lifted = signs * magnitude * jnp.exp(-steps / spans) * scale / jnp.sqrt(4.33 * energy)
    return (lifted - jnp.roll(lifted, 1, axis=1)).astype(jnp.float32)


def draw_key_proj(key, part):
    first, second = jax.random.split(jax.random.fold_in(key, 23), 2)
    centre = jax.random.uniform(first, (1, 1, CH), minval=2.2, maxval=2.8)
    noise = 0.45 * jnp.clip(jax.random.normal(second, (GENOMES, L, CH)), -4.4, 4.4)
    return (centre + noise).astype(jnp.bfloat16)


def draw_value_proj(key, part):
    first, second = jax.random.split(jax.random.fold_in(key, 37), 2)
    centre = jax.random.uniform(first, (1, 1, CH), minval=2.2, maxval=2.8)
    noise = 0.45 * jnp.clip(jax.random.normal(second, (GENOMES, L, CH)), -4.4, 4.4)
    return (centre + noise).astype(jnp.bfloat16)


def block_scale(own_key, shape, pieces, low, top_value):
    level, own = 1.0, jax.random.fold_in(own_key, 6)
    for dim, blocks in pieces:
        draws = jnp.exp(jax.random.uniform(jax.random.fold_in(own, dim), (blocks,), jnp.float32, low / len(pieces), top_value / len(pieces)))
        level = level * jnp.repeat(draws, shape[dim] // blocks).reshape([-1 if axis == dim else 1 for axis in range(len(shape))])
    return level


def bell_draw(key, extent, scale, limit, cuts=(), held_as=jnp.bfloat16):
    gain = block_scale(key, extent, cuts, -0.22, 0.18) if cuts else 1.0
    result = jax.random.normal(key, extent, jnp.float32) * scale * gain
    return jnp.minimum(jnp.maximum(result, -limit), limit).astype(held_as)


def setup_inputs(seed: int = 0) -> dict:
    streams_of = jax.random.split(jax.random.key(seed), 5)
    return {
        "query_proj": bell_draw(streams_of[0], (GENOMES, L, CH), 1.0, 6.0, ((0, 8), (1, 4))),
        "key_proj": draw_key_proj(jax.random.fold_in(streams_of[4], 71), 0),
        "value_proj": draw_value_proj(jax.random.fold_in(streams_of[4], 71), 0),
        "filters": draw_filters(jax.random.fold_in(streams_of[4], 71), 0),
    }


def causal_filter(padded, taps):
    length = padded.shape[0] - TAPS + 1

    def add_tap(index, total):
        offset = (TAPS - 1 - index).astype(jnp.int32)
        window = lax.dynamic_slice_in_dim(padded, offset, length, 0)
        weight = lax.dynamic_index_in_dim(taps, index.astype(jnp.int32), 1, keepdims=False)
        return total + weight[None, :] * window

    start = jnp.zeros((length, padded.shape[1]), jnp.float32)
    return lax.fori_loop(jnp.int32(0), jnp.int32(TAPS), add_tap, start)


def one_genome(operands):
    query_row, key_row, value_row, taps = operands
    mixed = (key_row.astype(jnp.float32) * value_row.astype(jnp.float32)).astype(jnp.bfloat16)
    padded = jnp.pad(mixed.astype(jnp.float32), ((TAPS - 1, 0), (0, 0)))
    filtered = causal_filter(padded, taps)
    return (query_row.astype(jnp.float32) * filtered).astype(jnp.bfloat16)


def reference(query_proj, key_proj, value_proj, filters):
    def single(items):
        return one_genome((items[0], items[1], items[2], filters))
    return lax.map(single, (query_proj, key_proj, value_proj))
```

```python
import functools

import jax
import jax.numpy as jnp
from jax import lax
from jax.experimental import pallas as pl
from jax.experimental.pallas import tpu as pltpu
from jax.sharding import PartitionSpec as P

MESH = pl.DeviceIdType.MESH
LANES = 128
SUB = 8


def kernel(nf, ns, q_hbm, k_hbm, v_hbm, f_hbm, out_ref, kb, vb, qb, mix, halo, taps, tapsT, pad,
           load_sem, tail_send, tail_recv, f_send, f_recv):
    fi = lax.axis_index("fsdp")
    si = lax.axis_index("seq")
    span, channels = kb.shape
    own, width = f_hbm.shape
    halo_rows = halo.shape[0]
    mine = pl.ds(pl.multiple_of(fi * own, own), own)

    load_f = pltpu.make_async_copy(f_hbm, taps.at[mine], load_sem.at[0])
    load_k = pltpu.make_async_copy(k_hbm.at[0], kb, load_sem.at[1])
    load_v = pltpu.make_async_copy(v_hbm.at[0], vb, load_sem.at[2])
    load_q = pltpu.make_async_copy(q_hbm.at[0], qb, load_sem.at[3])
    load_f.start()
    load_k.start()
    load_v.start()
    load_q.start()

    barrier = pltpu.get_barrier_semaphore()
    for step in range(1, nf):
        pl.semaphore_signal(barrier, inc=1, device_id=(lax.rem(fi + step, nf), si), device_id_type=MESH)

    @pl.when(si > 0)
    def _():
        pl.semaphore_signal(barrier, inc=1, device_id=(fi, si - 1), device_id_type=MESH)

    load_k.wait()
    load_v.wait()
    mix[...] = (kb[...].astype(jnp.float32) * vb[...].astype(jnp.float32)).astype(jnp.bfloat16)
    for c in range(channels // LANES):
        pad[c, halo_rows:, :] = mix[:, c * LANES:(c + 1) * LANES].astype(jnp.float32)
    load_f.wait()

    @pl.when(si < ns - 1)
    def _():
        pl.semaphore_wait(barrier, nf)

    @pl.when(si == ns - 1)
    def _():
        pl.semaphore_wait(barrier, nf - 1)

    sends = []
    for step in range(1, nf):
        copy = pltpu.make_async_remote_copy(
            src_ref=taps.at[mine], dst_ref=taps.at[mine], send_sem=f_send, recv_sem=f_recv,
            device_id=(lax.rem(fi + step, nf), si), device_id_type=MESH)
        copy.start()
        sends.append(copy)
    tail = pltpu.make_async_remote_copy(
        src_ref=mix.at[pl.ds(span - halo_rows, halo_rows)], dst_ref=halo, send_sem=tail_send, recv_sem=tail_recv,
        device_id=(fi, lax.rem(si + 1, ns)), device_id_type=MESH)

    @pl.when(si < ns - 1)
    def _():
        tail.start()

    load_q.wait()

    @pl.when(si > 0)
    def _():
        tail.wait_recv()
        for c in range(channels // LANES):
            pad[c, :halo_rows, :] = halo[:, c * LANES:(c + 1) * LANES].astype(jnp.float32)

    @pl.when(si == 0)
    def _():
        for c in range(channels // LANES):
            pad[c, :halo_rows, :] = jnp.zeros((halo_rows, LANES), jnp.float32)

    others = taps.at[pl.ds(0, channels - own)]
    pltpu.make_async_copy(others, others, f_recv).wait()

    groups = width // SUB
    tiles = span // SUB
    base = halo_rows // SUB
    for c in range(channels // LANES):
        tapsT[...] = taps[c * LANES:(c + 1) * LANES, :].T

        def phase(b, acc):
            acc = list(acc)
            weights = [jnp.broadcast_to(tapsT[pl.ds(a * SUB + b, 1), :], (SUB, LANES)) for a in range(groups)]
            for row in range(base - groups + 1, base + tiles):
                window = pad[c, pl.ds(row * SUB - b, SUB), :]
                for a in range(groups):
                    j = row - base + a
                    if 0 <= j < tiles:
                        acc[j] = acc[j] + weights[a] * window
            return tuple(acc)

        acc = lax.fori_loop(0, SUB, phase, tuple(jnp.zeros((SUB, LANES), jnp.float32) for _ in range(tiles)))
        cols = slice(c * LANES, (c + 1) * LANES)
        gate = qb[:, cols].astype(jnp.float32)
        out_ref[0, :, cols] = (gate * jnp.concatenate(acc, axis=0)).astype(jnp.bfloat16)

    pltpu.make_async_copy(others, others, f_send).wait()

    @pl.when(si < ns - 1)
    def _():
        tail.wait_send()


def solution(mesh):
    nf, ns = mesh.shape["fsdp"], mesh.shape["seq"]

    def per_device(query_proj, key_proj, value_proj, filters):
        _, span, channels = key_proj.shape
        own, width = filters.shape
        return pl.pallas_call(
            functools.partial(kernel, nf, ns),
            out_shape=jax.ShapeDtypeStruct(query_proj.shape, jnp.bfloat16),
            in_specs=[pl.BlockSpec(memory_space=pltpu.HBM)] * 4,
            out_specs=pl.BlockSpec(memory_space=pltpu.VMEM),
            scratch_shapes=[
                pltpu.VMEM((span, channels), jnp.bfloat16),
                pltpu.VMEM((span, channels), jnp.bfloat16),
                pltpu.VMEM((span, channels), jnp.bfloat16),
                pltpu.VMEM((span, channels), jnp.bfloat16),
                pltpu.VMEM((width, channels), jnp.bfloat16),
                pltpu.VMEM((channels, width), jnp.float32),
                pltpu.VMEM((width, LANES), jnp.float32),
                pltpu.VMEM((channels // LANES, width + span, LANES), jnp.float32),
                pltpu.SemaphoreType.DMA((4,)),
                pltpu.SemaphoreType.DMA,
                pltpu.SemaphoreType.DMA,
                pltpu.SemaphoreType.DMA,
                pltpu.SemaphoreType.DMA,
            ],
            compiler_params=pltpu.CompilerParams(collective_id=0, has_side_effects=True,
                                                 vmem_limit_bytes=40 * 1024 * 1024),
        )(query_proj, key_proj, value_proj, filters)

    in_specs = (P("fsdp", "seq", None),) * 3 + (P("fsdp", None),)
    return jax.shard_map(per_device, mesh=mesh, in_specs=in_specs, out_specs=P("fsdp", "seq", None), check_vma=False)
```

```python
import functools

import jax
import jax.numpy as jnp
from jax import lax
from jax.experimental import pallas as pl
from jax.experimental.pallas import tpu as pltpu
from jax.sharding import PartitionSpec as P

MESH = pl.DeviceIdType.MESH
LANES = 128
SUB = 8


def kernel(nf, ns, q_hbm, k_hbm, v_hbm, f_hbm, out_ref, kb, vb, qb, mix, halo, taps, tapsT, pad,
           load_sem, tail_send, tail_recv, f_send, f_recv):
    fi = lax.axis_index("fsdp")
    si = lax.axis_index("seq")
    span, channels = kb.shape
    own, width = f_hbm.shape
    halo_rows = halo.shape[0]
    mine = pl.ds(pl.multiple_of(fi * own, own), own)

    load_f = pltpu.make_async_copy(f_hbm, taps.at[mine], load_sem.at[0])
    load_k = pltpu.make_async_copy(k_hbm.at[0], kb, load_sem.at[1])
    load_v = pltpu.make_async_copy(v_hbm.at[0], vb, load_sem.at[2])
    load_q = pltpu.make_async_copy(q_hbm.at[0], qb, load_sem.at[3])
    load_f.start()
    load_k.start()
    load_v.start()
    load_q.start()

    barrier = pltpu.get_barrier_semaphore()
    for step in range(1, nf):
        pl.semaphore_signal(barrier, inc=1, device_id=(lax.rem(fi + step, nf), si), device_id_type=MESH)

    @pl.when(si > 0)
    def _():
        pl.semaphore_signal(barrier, inc=1, device_id=(fi, si - 1), device_id_type=MESH)

    load_k.wait()
    load_v.wait()
    mix[...] = (kb[...].astype(jnp.float32) * vb[...].astype(jnp.float32)).astype(jnp.bfloat16)
    for c in range(channels // LANES):
        pad[c, halo_rows:, :] = mix[:, c * LANES:(c + 1) * LANES].astype(jnp.float32)
    load_f.wait()

    @pl.when(si < ns - 1)
    def _():
        pl.semaphore_wait(barrier, nf)

    @pl.when(si == ns - 1)
    def _():
        pl.semaphore_wait(barrier, nf - 1)

    sends = []
    for step in range(1, nf):
        copy = pltpu.make_async_remote_copy(
            src_ref=taps.at[mine], dst_ref=taps.at[mine], send_sem=f_send, recv_sem=f_recv,
            device_id=(lax.rem(fi + step, nf), si), device_id_type=MESH)
        copy.start()
        sends.append(copy)
    tail = pltpu.make_async_remote_copy(
        src_ref=mix.at[pl.ds(span - halo_rows, halo_rows)], dst_ref=halo, send_sem=tail_send, recv_sem=tail_recv,
        device_id=(fi, lax.rem(si + 1, ns)), device_id_type=MESH)

    @pl.when(si < ns - 1)
    def _():
        tail.start()

    load_q.wait()

    @pl.when(si > 0)
    def _():
        tail.wait_recv()
        for c in range(channels // LANES):
            pad[c, :halo_rows, :] = halo[:, c * LANES:(c + 1) * LANES].astype(jnp.float32)

    @pl.when(si == 0)
    def _():
        for c in range(channels // LANES):
            pad[c, :halo_rows, :] = jnp.zeros((halo_rows, LANES), jnp.float32)

    others = taps.at[pl.ds(0, channels - own)]
    pltpu.make_async_copy(others, others, f_recv).wait()

    groups = width // SUB
    tiles = span // SUB
    base = halo_rows // SUB
    for c in range(channels // LANES):
        tapsT[...] = taps[c * LANES:(c + 1) * LANES, :].T

        def phase(b, acc):
            acc = list(acc)
            weights = [jnp.broadcast_to(tapsT[pl.ds(a * SUB + b, 1), :], (SUB, LANES)) for a in range(groups)]
            for row in range(base - groups + 1, base + tiles):
                window = pad[c, pl.ds(row * SUB - b, SUB), :]
                for a in range(groups):
                    j = row - base + a
                    if 0 <= j < tiles:
                        acc[j] = acc[j] + weights[a] * window
            return tuple(acc)

        acc = lax.fori_loop(0, SUB, phase, tuple(jnp.zeros((SUB, LANES), jnp.float32) for _ in range(tiles)))
        cols = slice(c * LANES, (c + 1) * LANES)
        gate = qb[:, cols].astype(jnp.float32)
        out_ref[0, :, cols] = (gate * jnp.concatenate(acc, axis=0)).astype(jnp.bfloat16)

    pltpu.make_async_copy(others, others, f_send).wait()

    @pl.when(si < ns - 1)
    def _():
        tail.wait_send()


def solution(mesh):
    nf, ns = mesh.shape["fsdp"], mesh.shape["seq"]

    def per_device(query_proj, key_proj, value_proj, filters):
        _, span, channels = key_proj.shape
        own, width = filters.shape
        return pl.pallas_call(
            functools.partial(kernel, nf, ns),
            out_shape=jax.ShapeDtypeStruct(query_proj.shape, jnp.bfloat16),
            in_specs=[pl.BlockSpec(memory_space=pltpu.HBM)] * 4,
            out_specs=pl.BlockSpec(memory_space=pltpu.VMEM),
            scratch_shapes=[
                pltpu.VMEM((span, channels), jnp.bfloat16),
                pltpu.VMEM((span, channels), jnp.bfloat16),
                pltpu.VMEM((span, channels), jnp.bfloat16),
                pltpu.VMEM((span, channels), jnp.bfloat16),
                pltpu.VMEM((width, channels), jnp.bfloat16),
                pltpu.VMEM((channels, width), jnp.float32),
                pltpu.VMEM((width, LANES), jnp.float32),
                pltpu.VMEM((channels // LANES, width + span, LANES), jnp.float32),
                pltpu.SemaphoreType.DMA((4,)),
                pltpu.SemaphoreType.DMA,
                pltpu.SemaphoreType.DMA,
                pltpu.SemaphoreType.DMA,
                pltpu.SemaphoreType.DMA,
            ],
            compiler_params=pltpu.CompilerParams(collective_id=0, has_side_effects=True,
                                                 vmem_limit_bytes=40 * 1024 * 1024),
        )(*[pltpu.with_memory_space_constraint(x, pltpu.HBM) for x in (query_proj, key_proj, value_proj, filters)])

    in_specs = (P("fsdp", "seq", None),) * 3 + (P("fsdp", None),)
    return jax.shard_map(per_device, mesh=mesh, in_specs=in_specs, out_specs=P("fsdp", "seq", None), check_vma=False)
```

```python
import functools

import jax
import jax.numpy as jnp
from jax import lax
from jax.experimental import pallas as pl
from jax.experimental.pallas import tpu as pltpu
from jax.sharding import PartitionSpec as P

MESH = pl.DeviceIdType.MESH
LANES = 128
SUB = 8


def partners(index, count):
    if count & (count - 1):
        return [lax.rem(index + step, count) for step in range(1, count)]
    found = []
    for mask in sorted(range(1, count), key=lambda mask: (-(mask // 2), mask)):
        other = index
        for bit in range(count.bit_length()):
            if mask >> bit & 1:
                other = other + (1 << bit) * (1 - 2 * (index // (1 << bit) % 2))
        found.append(other)
    return found


def kernel(nf, ns, group, q_hbm, k_hbm, v_hbm, f_hbm, out_ref, kb, vb, qb, fb, mix, halo, taps, tapsT, packed, gates,
           done, load_sem, tail_send, tail_recv, f_send, f_recv):
    fi = lax.axis_index("fsdp")
    si = lax.axis_index("seq")
    span, channels = kb.shape
    own, width = f_hbm.shape
    groups, _, _ = packed.shape
    parts = LANES // group
    rows = span // parts
    mine = pl.ds(pl.multiple_of(fi * own, own), own)
    my_group = fi * own // group

    peers = partners(fi, nf)

    barrier = pltpu.get_barrier_semaphore()
    for peer in peers:
        pl.semaphore_signal(barrier, inc=1, device_id=(peer, si), device_id_type=MESH)

    @pl.when(si > 0)
    def _():
        pl.semaphore_signal(barrier, inc=1, device_id=(fi, si - 1), device_id_type=MESH)

    load_f = pltpu.make_async_copy(f_hbm, fb, load_sem.at[0])
    load_k = pltpu.make_async_copy(k_hbm.at[0], kb, load_sem.at[1])
    load_v = pltpu.make_async_copy(v_hbm.at[0], vb, load_sem.at[2])
    load_q = pltpu.make_async_copy(q_hbm.at[0], qb, load_sem.at[3])
    load_f.start()
    load_k.start()
    load_v.start()
    load_q.start()
    pltpu.make_async_copy(f_hbm, taps.at[mine], f_recv.at[my_group]).start()

    load_k.wait()
    load_v.wait()
    mix[...] = (kb[...].astype(jnp.float32) * vb[...].astype(jnp.float32)).astype(jnp.bfloat16)
    load_f.wait()

    @pl.when(si < ns - 1)
    def _():
        pl.semaphore_wait(barrier, nf)

    @pl.when(si == ns - 1)
    def _():
        pl.semaphore_wait(barrier, nf - 1)

    for peer in peers:
        pltpu.make_async_remote_copy(
            src_ref=fb, dst_ref=taps.at[mine], send_sem=f_send, recv_sem=f_recv.at[my_group],
            device_id=(peer, si), device_id_type=MESH).start()
    tail = pltpu.make_async_remote_copy(
        src_ref=mix.at[pl.ds(span - width, width)], dst_ref=halo, send_sem=tail_send, recv_sem=tail_recv,
        device_id=(fi, lax.rem(si + 1, ns)), device_id_type=MESH)

    @pl.when(si < ns - 1)
    def _():
        tail.start()

    def pack(first, block):
        for k in range(block.shape[1] // group):
            for h in range(parts):
                low, high = max(first, h * rows), min(first + block.shape[0], h * rows + width + rows)
                piece = block[low - first:high - first, k * group:(k + 1) * group]
                packed[k, low - h * rows:high - h * rows, h * group:(h + 1) * group] = piece

    pack(width, mix[...].astype(jnp.float32))
    load_q.wait()
    gate = qb[...].astype(jnp.float32)
    for k in range(groups):
        for h in range(parts):
            piece = gate[h * rows:(h + 1) * rows, k * group:(k + 1) * group]
            gates[k, :, h * group:(h + 1) * group] = piece

    @pl.when(si > 0)
    def _():
        tail.wait_recv()
        pack(0, halo[...].astype(jnp.float32))

    @pl.when(si == 0)
    def _():
        pack(0, jnp.zeros(halo.shape, jnp.float32))

    tiles = rows // SUB
    spread = width // SUB
    upper = (my_group * 2) // groups

    def one_group(order, carry):
        g = order + upper * (groups - 1 - 2 * order)
        block = taps.at[pl.ds(pl.multiple_of(g * group, group), group)]
        pltpu.make_async_copy(block, block, f_recv.at[g]).wait()
        tapsT[...] = jnp.concatenate([block[...]] * parts, axis=0).T
        acc = [[jnp.zeros((SUB, LANES), jnp.float32) for _ in range(tiles)] for _ in range(4)]
        for b in range(SUB):
            weights = [jnp.broadcast_to(tapsT[a * SUB + b:a * SUB + b + 1, :], (SUB, LANES)) for a in range(spread)]
            for row in range(1, spread + tiles):
                window = packed[g, row * SUB - b:row * SUB - b + SUB, :]
                for a in range(spread):
                    j = row - spread + a
                    if 0 <= j < tiles:
                        acc[a % 4][j] = acc[a % 4][j] + weights[a] * window
        total = jnp.concatenate([(p + q) + (r + s) for p, q, r, s in zip(*acc)], axis=0)
        done[g] = total * gates[g]
        return carry

    lax.fori_loop(0, groups, one_group, 0)

    for c in range(channels // LANES):
        for h in range(parts):
            pieces = [done[c * parts + k, :, h * group:(h + 1) * group] for k in range(parts)]
            out_ref[0, h * rows:(h + 1) * rows, c * LANES:(c + 1) * LANES] = (
                jnp.concatenate(pieces, axis=1).astype(jnp.bfloat16))

    others = taps.at[pl.ds(0, channels - own)]
    pltpu.make_async_copy(others, others, f_send).wait()

    @pl.when(si < ns - 1)
    def _():
        tail.wait_send()


def solution(mesh):
    nf, ns = mesh.shape["fsdp"], mesh.shape["seq"]

    def per_device(query_proj, key_proj, value_proj, filters):
        _, span, channels = key_proj.shape
        own, width = filters.shape
        group = max(own, 32)
        groups, rows = channels // group, span * group // LANES
        operands = [pltpu.with_memory_space_constraint(x, pltpu.HBM)
                    for x in (query_proj, key_proj, value_proj, filters)]
        return pl.pallas_call(
            functools.partial(kernel, nf, ns, group),
            out_shape=jax.ShapeDtypeStruct(query_proj.shape, jnp.bfloat16),
            in_specs=[pl.BlockSpec(memory_space=pltpu.HBM)] * 4,
            out_specs=pl.BlockSpec(memory_space=pltpu.VMEM),
            scratch_shapes=[
                pltpu.VMEM((span, channels), jnp.bfloat16),
                pltpu.VMEM((span, channels), jnp.bfloat16),
                pltpu.VMEM((span, channels), jnp.bfloat16),
                pltpu.VMEM((own, width), jnp.float32),
                pltpu.VMEM((span, channels), jnp.bfloat16),
                pltpu.VMEM((width, channels), jnp.bfloat16),
                pltpu.VMEM((channels, width), jnp.float32),
                pltpu.VMEM((width, LANES), jnp.float32),
                pltpu.VMEM((groups, width + rows, LANES), jnp.float32),
                pltpu.VMEM((groups, rows, LANES), jnp.float32),
                pltpu.VMEM((groups, rows, LANES), jnp.float32),
                pltpu.SemaphoreType.DMA((4,)),
                pltpu.SemaphoreType.DMA,
                pltpu.SemaphoreType.DMA,
                pltpu.SemaphoreType.DMA,
                pltpu.SemaphoreType.DMA((groups,)),
            ],
            compiler_params=pltpu.CompilerParams(collective_id=0, has_side_effects=True,
                                                 vmem_limit_bytes=40 * 1024 * 1024),
        )(*operands)

    in_specs = (P("fsdp", "seq", None),) * 3 + (P("fsdp", None),)
    return jax.shard_map(per_device, mesh=mesh, in_specs=in_specs, out_specs=P("fsdp", "seq", None), check_vma=False)
```

```python
import functools

import jax
import jax.numpy as jnp
from jax import lax
from jax.experimental import pallas as pl
from jax.experimental.pallas import tpu as pltpu
from jax.sharding import PartitionSpec as P

MESH = pl.DeviceIdType.MESH
LANES = 128
SUB = 8


def partners(index, count):
    if count & (count - 1):
        return [lax.rem(index + step, count) for step in range(1, count)]
    found = []
    for mask in sorted(range(1, count), key=lambda mask: (-(mask // 2), mask)):
        other = index
        for bit in range(count.bit_length()):
            if mask >> bit & 1:
                other = other + (1 << bit) * (1 - 2 * (index // (1 << bit) % 2))
        found.append(other)
    return found


def kernel(nf, ns, group, q_hbm, k_hbm, v_hbm, f_hbm, out_ref, kb, vb, qb, fb, mix, halo, taps, packed, gates,
           done, load_sem, tail_send, tail_recv, f_send, f_recv):
    fi = lax.axis_index("fsdp")
    si = lax.axis_index("seq")
    span, channels = kb.shape
    own, width = f_hbm.shape
    groups, _, _ = packed.shape
    parts = LANES // group
    rows = span // parts
    mine = pl.ds(pl.multiple_of(fi * own, own), own)
    my_group = fi * own // group

    peers = partners(fi, nf)

    barrier = pltpu.get_barrier_semaphore()
    for peer in peers:
        pl.semaphore_signal(barrier, inc=1, device_id=(peer, si), device_id_type=MESH)

    @pl.when(si > 0)
    def _():
        pl.semaphore_signal(barrier, inc=1, device_id=(fi, si - 1), device_id_type=MESH)

    load_f = pltpu.make_async_copy(f_hbm, fb, load_sem.at[0])
    load_k = pltpu.make_async_copy(k_hbm.at[0], kb, load_sem.at[1])
    load_v = pltpu.make_async_copy(v_hbm.at[0], vb, load_sem.at[2])
    load_q = pltpu.make_async_copy(q_hbm.at[0], qb, load_sem.at[3])
    load_f.start()
    load_k.start()
    load_v.start()
    load_q.start()
    pltpu.make_async_copy(f_hbm, taps.at[mine], f_recv.at[my_group]).start()

    load_k.wait()
    load_v.wait()
    mix[...] = (kb[...].astype(jnp.float32) * vb[...].astype(jnp.float32)).astype(jnp.bfloat16)
    load_f.wait()

    @pl.when(si < ns - 1)
    def _():
        pl.semaphore_wait(barrier, nf)

    @pl.when(si == ns - 1)
    def _():
        pl.semaphore_wait(barrier, nf - 1)

    for peer in peers[:4]:
        pltpu.make_async_remote_copy(
            src_ref=fb, dst_ref=taps.at[mine], send_sem=f_send, recv_sem=f_recv.at[my_group],
            device_id=(peer, si), device_id_type=MESH).start()

    tail = pltpu.make_async_remote_copy(
        src_ref=mix.at[pl.ds(span - width, width)], dst_ref=halo, send_sem=tail_send, recv_sem=tail_recv,
        device_id=(fi, lax.rem(si + 1, ns)), device_id_type=MESH)

    @pl.when(si < ns - 1)
    def _():
        tail.start()

    for peer in peers[4:]:
        pltpu.make_async_remote_copy(
            src_ref=fb, dst_ref=taps.at[mine], send_sem=f_send, recv_sem=f_recv.at[my_group],
            device_id=(peer, si), device_id_type=MESH).start()

    def pack(first, block):
        for k in range(block.shape[1] // group):
            for h in range(parts):
                low, high = max(first, h * rows), min(first + block.shape[0], h * rows + width + rows)
                piece = block[low - first:high - first, k * group:(k + 1) * group]
                packed[k, low - h * rows:high - h * rows, h * group:(h + 1) * group] = piece

    pack(width, mix[...].astype(jnp.float32))
    load_q.wait()
    gate = qb[...].astype(jnp.float32)
    for k in range(groups):
        for h in range(parts):
            piece = gate[h * rows:(h + 1) * rows, k * group:(k + 1) * group]
            gates[k, :, h * group:(h + 1) * group] = piece

    @pl.when(si > 0)
    def _():
        tail.wait_recv()
        pack(0, halo[...].astype(jnp.float32))

    @pl.when(si == 0)
    def _():
        pack(0, jnp.zeros(halo.shape, jnp.float32))

    tiles = rows // SUB
    spread = width // SUB
    upper = (my_group * 2) // groups

    def one_group(order, carry):
        g = order + upper * (groups - 1 - 2 * order)
        block = taps.at[pl.ds(pl.multiple_of(g * group, group), group)]
        pltpu.make_async_copy(block, block, f_recv.at[g]).wait()
        turned = jnp.concatenate([block[...]] * parts, axis=0).T
        acc = [[jnp.zeros((SUB, LANES), jnp.float32) for _ in range(tiles)] for _ in range(4)]
        for b in range(SUB):
            weights = [jnp.broadcast_to(turned[a * SUB + b:a * SUB + b + 1, :], (SUB, LANES)) for a in range(spread)]
            for row in range(1, spread + tiles):
                window = packed[g, row * SUB - b:row * SUB - b + SUB, :]
                for a in range(spread):
                    j = row - spread + a
                    if 0 <= j < tiles:
                        acc[a % 4][j] = acc[a % 4][j] + weights[a] * window
        total = jnp.concatenate([(p + q) + (r + s) for p, q, r, s in zip(*acc)], axis=0)
        done[g] = total * gates[g]
        return carry

    lax.fori_loop(0, groups, one_group, 0)

    for c in range(channels // LANES):
        for h in range(parts):
            pieces = [done[c * parts + k, :, h * group:(h + 1) * group] for k in range(parts)]
            out_ref[0, h * rows:(h + 1) * rows, c * LANES:(c + 1) * LANES] = (
                jnp.concatenate(pieces, axis=1).astype(jnp.bfloat16))

    others = taps.at[pl.ds(0, channels - own)]
    pltpu.make_async_copy(others, others, f_send).wait()

    @pl.when(si < ns - 1)
    def _():
        tail.wait_send()


def solution(mesh):
    nf, ns = mesh.shape["fsdp"], mesh.shape["seq"]

    def per_device(query_proj, key_proj, value_proj, filters):
        _, span, channels = key_proj.shape
        own, width = filters.shape
        group = max(own, 32)
        groups, rows = channels // group, span * group // LANES
        operands = [pltpu.with_memory_space_constraint(x, pltpu.HBM)
                    for x in (query_proj, key_proj, value_proj, filters)]
        return pl.pallas_call(
            functools.partial(kernel, nf, ns, group),
            out_shape=jax.ShapeDtypeStruct(query_proj.shape, jnp.bfloat16),
            in_specs=[pl.BlockSpec(memory_space=pltpu.HBM)] * 4,
            out_specs=pl.BlockSpec(memory_space=pltpu.VMEM),
            scratch_shapes=[
                pltpu.VMEM((span, channels), jnp.bfloat16),
                pltpu.VMEM((span, channels), jnp.bfloat16),
                pltpu.VMEM((span, channels), jnp.bfloat16),
                pltpu.VMEM((own, width), jnp.float32),
                pltpu.VMEM((span, channels), jnp.bfloat16),
                pltpu.VMEM((width, channels), jnp.bfloat16),
                pltpu.VMEM((channels, width), jnp.float32),
                pltpu.VMEM((groups, width + rows, LANES), jnp.float32),
                pltpu.VMEM((groups, rows, LANES), jnp.float32),
                pltpu.VMEM((groups, rows, LANES), jnp.float32),
                pltpu.SemaphoreType.DMA((4,)),
                pltpu.SemaphoreType.DMA,
                pltpu.SemaphoreType.DMA,
                pltpu.SemaphoreType.DMA,
                pltpu.SemaphoreType.DMA((groups,)),
            ],
            compiler_params=pltpu.CompilerParams(collective_id=0, has_side_effects=True,
                                                 vmem_limit_bytes=40 * 1024 * 1024),
        )(*operands)

    in_specs = (P("fsdp", "seq", None),) * 3 + (P("fsdp", None),)
    return jax.shard_map(per_device, mesh=mesh, in_specs=in_specs, out_specs=P("fsdp", "seq", None), check_vma=False)
```
